32 devices in a mesh: grp: 4 (over y, x), pen: 8 (over z, core).
Axes of the slice: x: 2, y: 2, z: 4, core: 2. Of those that a mesh axis runs over, the one named last changes fastest.
Arguments:
- columns: float32 [2, 512, 512, 512], P(None, 'grp', 'pen'), may hold values from -6 to 6
- basis_in_x: float32 [512, 512], replicated, may hold values from -0.25 to 0.25
- basis_in_y: float32 [512, 512], replicated, may hold values from -0.25 to 0.25
- basis_in_z: float32 [512, 512], replicated, may hold values from -0.25 to 0.25
- basis_out_x: float32 [512, 512], replicated, may hold values from -0.25 to 0.25
- basis_out_y: float32 [512, 512], replicated, may hold values from -0.25 to 0.25
- basis_out_z: float32 [512, 512], replicated, may hold values from -0.25 to 0.25
- eig_x: float32 [512], replicated, may hold values from 0.05 to 3
- eig_y: float32 [512], replicated, may hold values from 0.05 to 3
- eig_z: float32 [512], replicated, may hold values from 0.05 to 3
- shift_table: float32 [64], replicated, may hold values from 0.5 to 8
- shift_index: int32 [2], replicated, may hold values from 0 to 63
Outputs:
- solved: float32 [2, 512, 512, 512], P(None, 'grp', 'pen')
The draws below stay inside these ranges and needn't reach their ends.
Inputs may be any that keep to these rules, and one draw needn't show every extreme that they name: `shift_index`: indices into shift_table.
All inputs are finite; a program needn't handle non-finite values.
Results may differ from the reference program's by a relative error of at most 0.00007.
Values sent between devices are 32-bit elements; how exact they have to be, the bound alone decides.
No kernel may reach another device: no remote copies, remote signals or barrier semaphores. Data moves between devices by JAX's collectives and lax.ppermute only.
A program may use at most 256 MiB of HBM per device.

```python
import math
import jax
import jax.numpy as jnp
from jax import lax

N = 512
COLS = 2
NSHIFT = 64


def shard_levels(key, dims, pieces, low, largest):
    def one(position, blocks):
        draws = jax.random.uniform(jax.random.fold_in(jax.random.fold_in(key, 6), position), (blocks,), jnp.float32, low / len(pieces), largest / len(pieces))
        return jnp.repeat(jnp.exp(draws), dims[position] // blocks).reshape((-1,) + (1,) * (len(dims) - position - 1))

    loudness = one(*pieces[0])
    for cut in pieces[1:]:
        loudness = loudness * one(*cut)
    return loudness


def centred(stream_key, shape, spread, bound, cuts=(), kind=jnp.bfloat16):
    level = shard_levels(stream_key, shape, cuts, -0.22, 0.18) if cuts else 1.0
    values = jax.random.normal(stream_key, shape, jnp.float32) * spread * level
    return jnp.minimum(jnp.maximum(values, -bound), bound).astype(kind)


def setup_inputs(seed: int = 0) -> dict:
    keys = jax.random.split(jax.random.key(seed), 13)
    return {
        "columns": centred(keys[0], (COLS, N, N, N), 1.0, 6.0, ((1, 4), (2, 8)), jnp.float32),
        "basis_in_x": centred(keys[1], (N, N), N ** -0.5, 0.25, (), jnp.float32),
        "basis_in_y": centred(keys[2], (N, N), N ** -0.5, 0.25, (), jnp.float32),
        "basis_in_z": centred(keys[3], (N, N), N ** -0.5, 0.25, (), jnp.float32),
        "basis_out_x": centred(keys[4], (N, N), N ** -0.5, 0.25, (), jnp.float32),
        "basis_out_y": centred(keys[5], (N, N), N ** -0.5, 0.25, (), jnp.float32),
        "basis_out_z": centred(keys[6], (N, N), N ** -0.5, 0.25, (), jnp.float32),
        "eig_x": jnp.clip(jnp.exp(jax.random.uniform(keys[7], (N,), jnp.float32, math.log(0.05), math.log(3.0))), 0.05, 3.0),
        "eig_y": jnp.clip(jnp.exp(jax.random.uniform(keys[8], (N,), jnp.float32, math.log(0.05), math.log(3.0))), 0.05, 3.0),
        "eig_z": jnp.clip(jnp.exp(jax.random.uniform(keys[9], (N,), jnp.float32, math.log(0.05), math.log(3.0))), 0.05, 3.0),
        "shift_table": jnp.clip(jnp.exp(jax.random.uniform(keys[10], (NSHIFT,), jnp.float32, math.log(0.5), math.log(8.0))), 0.5, 8.0),
        "shift_index": jax.random.randint(keys[11], (COLS,), 0, NSHIFT).astype(jnp.int32),
    }


def reference(columns, basis_in_x, basis_in_y, basis_in_z, basis_out_x, basis_out_y, basis_out_z, eig_x, eig_y, eig_z, shift_table, shift_index):
    highest = lax.Precision.HIGHEST
    shift_values = shift_table[shift_index]
    eig_sum = eig_x[:, None, None] + eig_y[None, :, None] + eig_z[None, None, :]

    def solve_one(pair):
        column, shift_value = pair
        scaling = jnp.sqrt(2.0 * shift_value)
        spectral = jnp.einsum('ix,xyz->iyz', basis_in_x, column, precision=highest)
        spectral = jnp.einsum('jy,iyz->ijz', basis_in_y, spectral, precision=highest)
        spectral = jnp.einsum('kz,ijz->ijk', basis_in_z, spectral, precision=highest)
        scaled = scaling * spectral / (eig_sum + shift_value)
        result = jnp.einsum('xi,ijk->xjk', basis_out_x, scaled, precision=highest)
        result = jnp.einsum('yj,xjk->xyk', basis_out_y, result, precision=highest)
        result = jnp.einsum('zk,xyk->xyz', basis_out_z, result, precision=highest)
        return result
    return lax.map(solve_one, (columns, shift_values))
```

```python
import jax
import jax.numpy as jnp
from jax import lax
from jax.experimental import pallas as pl
from jax.experimental.pallas import tpu as pltpu
from jax.sharding import PartitionSpec as P

CHUNKS = 1
LANES = 128
ROWS = 8
VMEM = 56 * 2**20
F32, BF16 = jnp.float32, jnp.bfloat16
BOTH = ("grp", "pen")


def table_parts(table, axis):
    high = lax.reduce_precision(table, exponent_bits=8, mantissa_bits=7)
    low = (table - high).astype(BF16)
    high = high.astype(BF16)
    return jnp.concatenate([high, low, high], axis=axis)


def data_parts(data, axis):
    high = data.astype(BF16)
    low = (data - high.astype(F32)).astype(BF16)
    return jnp.concatenate([high, high, low], axis=axis)


def contract(a, b, dims=((1,), (0,))):
    return lax.dot_general(a, b, (dims, ((), ())), preferred_element_type=F32)


def cost(flops, arrays):
    return pl.CostEstimate(
        flops=flops, bytes_accessed=sum(4 * a.size for a in arrays), transcendentals=0
    )


def params():
    return pltpu.CompilerParams(
        dimension_semantics=("arbitrary",), vmem_limit_bytes=VMEM
    )


def whole(shape):
    return pl.BlockSpec(shape, lambda i: (0,) * len(shape))


def z_in(columns, column, table, members):
    _, x_size, y_size, length = columns.shape
    rows, triple = table.shape
    part, tiles = rows // members, length // LANES
    out = jax.ShapeDtypeStruct((members, part, y_size, x_size), F32)

    def body(*refs):
        flat = [r.at[0].reshape(x_size * ROWS, LANES) for r in refs[:tiles]]
        tab, out = refs[tiles], refs[tiles + 1].reshape(rows * ROWS, x_size)
        for y in range(0, ROWS, 2):
            pair = jnp.concatenate(
                [
                    jnp.concatenate(
                        [f[pl.ds(y + d, x_size, stride=ROWS), :] for f in flat], axis=1
                    )
                    for d in range(2)
                ],
                axis=0,
            )
            done = contract(tab[...], data_parts(pair, 1), ((1,), (1,)))
            for d in range(2):
                out[pl.ds(y + d, rows, stride=ROWS), :] = done[
                    :, d * x_size : (d + 1) * x_size
                ]

    def tile(t):
        return pl.BlockSpec((1, x_size, ROWS, LANES), lambda i: (column, 0, i, t))

    return pl.pallas_call(
        body,
        grid=(y_size // ROWS,),
        in_specs=[tile(t) for t in range(tiles)] + [whole(table.shape)],
        out_specs=pl.BlockSpec((members, part, ROWS, x_size), lambda i: (0, 0, i, 0)),
        out_shape=out,
        compiler_params=params(),
        cost_estimate=cost(2 * rows * triple * x_size * y_size, [columns[0], out]),
    )(*[columns] * tiles, table)


def planes(blocks, groups, tables, eig_x, eig_y, eig_z, shift):
    members, k_size, y_size, x_size = blocks.shape
    slots = members // groups
    length = slots * y_size
    triple = 3 * length

    def body(data, y_in, x_in, x_out, y_out, ex, ey, ez, sh, out):
        plane = jnp.concatenate(
            [
                jnp.concatenate(
                    [data[g * slots + p, 0] for p in range(slots)], axis=0
                )
                for g in range(groups)
            ],
            axis=1,
        )
        spectral = contract(y_in[...], data_parts(plane, 0))
        spectral = contract(data_parts(spectral, 1), x_in[...])
        value = sh[0]
        root = jnp.sqrt(2.0 * jnp.full((1, length), value, F32))
        denominator = (ex[...] + ey[...]) + (ez[pl.program_id(0)] + value)
        scaled = root * spectral / denominator
        back = contract(data_parts(scaled, 1), x_out[...])
        back = contract(y_out[...], data_parts(back, 0))
        for g in range(groups):
            for p in range(slots):
                out[g * slots + p, 0] = back[
                    p * y_size : (p + 1) * y_size, g * x_size : (g + 1) * x_size
                ]

    block = pl.BlockSpec((members, 1, y_size, x_size), lambda i: (0, i, 0, 0))
    smem = pl.BlockSpec(memory_space=pltpu.SMEM)
    return pl.pallas_call(
        body,
        grid=(k_size,),
        in_specs=[block]
        + [whole(t.shape) for t in tables]
        + [whole((1, length)), whole((length, 1)), smem, smem],
        out_specs=block,
        out_shape=jax.ShapeDtypeStruct(blocks.shape, F32),
        compiler_params=params(),
        cost_estimate=cost(8 * triple * length * length * k_size, [blocks, blocks]),
    )(
        blocks,
        *tables,
        eig_x.reshape(1, length),
        eig_y.reshape(length, 1),
        eig_z,
        shift.reshape(1),
    )


def z_out(chunks, table, column, shape, earlier):
    members, part, y_size, x_size = chunks[0].shape
    triple, length = table.shape
    tiles, count, rows = length // LANES, len(chunks), members * part

    def body(*refs):
        flat = [r.reshape(rows * ROWS, x_size) for r in refs[:count]]
        tab, out, turned = refs[count], refs[-2], refs[-1]
        for y in range(0, ROWS, 2):
            pair = jnp.concatenate(
                [
                    jnp.concatenate(
                        [f[pl.ds(y + d, rows, stride=ROWS), :] for f in flat], axis=0
                    )
                    for d in range(2)
                ],
                axis=1,
            )
            done = contract(data_parts(pair.T, 1), tab[...])
            for d in range(2):
                for t in range(tiles):
                    turned[t, pl.ds(y + d, x_size, stride=ROWS), :] = done[
                        d * x_size : (d + 1) * x_size, t * LANES : (t + 1) * LANES
                    ]
        for t in range(tiles):
            out[0, :, :, t * LANES : (t + 1) * LANES] = turned[t].reshape(
                x_size, ROWS, LANES
            )

    given = [] if earlier is None else [earlier]
    return pl.pallas_call(
        body,
        grid=(y_size // ROWS,),
        in_specs=[
            pl.BlockSpec((members, part, ROWS, x_size), lambda i: (0, 0, i, 0))
        ]
        * count
        + [whole(table.shape)]
        + [pl.BlockSpec(memory_space=pl.ANY)] * len(given),
        out_specs=pl.BlockSpec((1, x_size, ROWS, length), lambda i: (column, 0, i, 0)),
        out_shape=jax.ShapeDtypeStruct(shape, F32),
        scratch_shapes=[pltpu.VMEM((tiles, x_size * ROWS, LANES), F32)],
        input_output_aliases={count + 1: 0} if given else {},
        compiler_params=params(),
        cost_estimate=cost(
            2 * triple * length * x_size * y_size, [*chunks, *chunks]
        ),
    )(*chunks, table, *given)


def z_in_plain(columns, column, table, members):
    exact = dict(precision=lax.Precision.HIGHEST)
    done = jnp.einsum("kz,xyz->kyx", table, columns[column], **exact)
    return done.reshape(members, -1, *done.shape[1:])


def planes_plain(blocks, groups, tables, eig_x, eig_y, eig_z, shift):
    exact = dict(precision=lax.Precision.HIGHEST)
    y_in, x_in, x_out, y_out = tables
    members, k_size, y_size, x_size = blocks.shape
    data = blocks.reshape(groups, members // groups, k_size, y_size, x_size)
    plane = data.transpose(2, 1, 3, 0, 4).reshape(
        k_size, members // groups * y_size, groups * x_size
    )
    spectral = jnp.einsum("jy,kyx->kjx", y_in, plane, **exact)
    spectral = jnp.einsum("kjx,xi->kji", spectral, x_in, **exact)
    denominator = eig_x[None, None] + eig_y[None, :, None] + eig_z[:, None, None] + shift
    scaled = jnp.sqrt(2.0 * shift) * spectral / denominator
    back = jnp.einsum("kji,ix->kjx", scaled, x_out, **exact)
    back = jnp.einsum("yj,kjx->kyx", y_out, back, **exact)
    back = back.reshape(k_size, members // groups, y_size, groups, x_size)
    return back.transpose(3, 1, 0, 2, 4).reshape(blocks.shape)


def z_out_plain(chunks, table, column, shape, earlier):
    exact = dict(precision=lax.Precision.HIGHEST)
    rows = jnp.concatenate([c.reshape(-1, *c.shape[2:]) for c in chunks])
    done = jnp.einsum("kyx,kz->xyz", rows, table, **exact)
    result = jnp.zeros(shape, F32) if earlier is None else earlier
    return result.at[column].set(done)


def per_device(
    columns,
    basis_in_x,
    basis_in_y,
    basis_in_z,
    basis_out_x,
    basis_out_y,
    basis_out_z,
    eig_x,
    eig_y,
    eig_z,
    shift_table,
    shift_index,
):
    count, x_size, y_size, length = columns.shape
    slots, groups = lax.axis_size("pen"), lax.axis_size("grp")
    members = slots * groups
    k_size = length // members
    chunks = CHUNKS if k_size % CHUNKS == 0 else 1
    chunk = k_size // chunks
    shift = shift_table[shift_index]
    tiled = x_size % LANES == 0 and y_size % ROWS == 0 and length % LANES == 0
    parts = table_parts if tiled else lambda table, axis: table
    to_z, across, from_z = (
        (z_in, planes, z_out) if tiled else (z_in_plain, planes_plain, z_out_plain)
    )

    rows = basis_in_z.reshape(members, chunks, chunk, length)
    in_tables = [parts(rows[:, m].reshape(-1, length), 1) for m in range(chunks)]
    cols = basis_out_z.T.reshape(members, chunks, chunk, length)
    out_table = parts(cols.transpose(1, 0, 2, 3).reshape(length, length), 0)
    tables = [
        parts(basis_in_y, 1),
        parts(basis_in_x.T, 0),
        parts(basis_out_x.T, 0),
        parts(basis_out_y, 1),
    ]
    first = lax.axis_index(BOTH) * k_size

    def exchange(blocks):
        return lax.all_to_all(blocks, BOTH, split_axis=0, concat_axis=0, tiled=True)

    units = [(c, m) for c in range(count) for m in range(chunks)]
    there = [exchange(to_z(columns, c, in_tables[m], members)) for c, m in units]
    back = []
    for (c, m), blocks in zip(units, there):
        levels = lax.dynamic_slice_in_dim(eig_z, first + m * chunk, chunk)
        back.append(
            exchange(across(blocks, groups, tables, eig_x, eig_y, levels, shift[c]))
        )
    result = None
    for c in range(count):
        mine = back[c * chunks : (c + 1) * chunks]
        result = from_z(mine, out_table, c, columns.shape, result)
    return result


def solution(mesh):
    in_specs = (P(None, "grp", "pen", None), P(), P(), P(), P(), P(), P(), P(), P(), P(), P(), P())
    out_specs = P(None, "grp", "pen", None)
    return jax.shard_map(
        per_device, mesh=mesh, in_specs=in_specs, out_specs=out_specs, check_vma=False
    )
```

```python
import jax
import jax.numpy as jnp
from jax import lax
from jax.experimental import pallas as pl
from jax.experimental.pallas import tpu as pltpu
from jax.sharding import PartitionSpec as P

END = 8
LANES = 128
ROWS = 8
VMEM = 56 * 2**20
F32, BF16 = jnp.float32, jnp.bfloat16
BOTH = ("grp", "pen")


def table_parts(table, axis):
    high = lax.reduce_precision(table, exponent_bits=8, mantissa_bits=7)
    low = (table - high).astype(BF16)
    high = high.astype(BF16)
    return jnp.concatenate([high, low, high], axis=axis)


def data_parts(data, axis):
    high = data.astype(BF16)
    low = (data - high.astype(F32)).astype(BF16)
    return jnp.concatenate([high, high, low], axis=axis)


def contract(a, b, dims=((1,), (0,))):
    return lax.dot_general(a, b, (dims, ((), ())), preferred_element_type=F32)


def cost(flops, arrays):
    return pl.CostEstimate(
        flops=flops, bytes_accessed=sum(4 * a.size for a in arrays), transcendentals=0
    )


def params():
    return pltpu.CompilerParams(
        dimension_semantics=("arbitrary",), vmem_limit_bytes=VMEM
    )


def whole(shape):
    return pl.BlockSpec(shape, lambda i: (0,) * len(shape))


def z_in(columns, column, table, members, first, y_size):
    _, x_size, _, length = columns.shape
    rows, triple = table.shape
    part, tiles, skip = rows // members, length // LANES, first // ROWS
    out = jax.ShapeDtypeStruct((members, part, y_size, x_size), F32)

    def body(*refs):
        flat = [r.at[0].reshape(x_size * ROWS, LANES) for r in refs[:tiles]]
        tab, out = refs[tiles], refs[tiles + 1].reshape(rows * ROWS, x_size)
        for y in range(0, ROWS, 2):
            pair = jnp.concatenate(
                [
                    jnp.concatenate(
                        [f[pl.ds(y + d, x_size, stride=ROWS), :] for f in flat], axis=1
                    )
                    for d in range(2)
                ],
                axis=0,
            )
            done = contract(tab[...], data_parts(pair, 1), ((1,), (1,)))
            for d in range(2):
                out[pl.ds(y + d, rows, stride=ROWS), :] = done[
                    :, d * x_size : (d + 1) * x_size
                ]

    def tile(t):
        return pl.BlockSpec(
            (1, x_size, ROWS, LANES), lambda i: (column, 0, i + skip, t)
        )

    return pl.pallas_call(
        body,
        grid=(y_size // ROWS,),
        in_specs=[tile(t) for t in range(tiles)] + [whole(table.shape)],
        out_specs=pl.BlockSpec((members, part, ROWS, x_size), lambda i: (0, 0, i, 0)),
        out_shape=out,
        compiler_params=params(),
        cost_estimate=cost(2 * rows * triple * x_size * y_size, [out, out]),
    )(*[columns] * tiles, table)


def planes(blocks, cuts, groups, tables, eig_x, eig_y, eig_z, shift):
    members, k_size, _, x_size = blocks[0].shape
    slots, count = members // groups, len(blocks)
    y_size = sum(b.shape[2] for b in blocks)
    length = slots * y_size
    triple = 3 * length

    def body(*refs):
        data, out = refs[:count], refs[count + 8 :]
        y_in, x_in, x_out, y_out, ex, ey, ez, sh = refs[count : count + 8]
        plane = jnp.concatenate(
            [
                jnp.concatenate(
                    [d[g * slots + p, 0] for p in range(slots) for d in data], axis=0
                )
                for g in range(groups)
            ],
            axis=1,
        )
        spectral = contract(y_in[...], data_parts(plane, 0))
        spectral = contract(data_parts(spectral, 1), x_in[...])
        value = sh[0]
        root = jnp.sqrt(2.0 * jnp.full((1, length), value, F32))
        denominator = (ex[...] + ey[...]) + (ez[pl.program_id(0)] + value)
        scaled = root * spectral / denominator
        back = contract(data_parts(scaled, 1), x_out[...])
        back = contract(y_out[...], data_parts(back, 0))
        for g in range(groups):
            for p in range(slots):
                start = p * y_size
                for o, cut in zip(out, cuts):
                    o[g * slots + p, 0] = back[
                        start : start + cut, g * x_size : (g + 1) * x_size
                    ]
                    start += cut

    def block(cut):
        return pl.BlockSpec((members, 1, cut, x_size), lambda i: (0, i, 0, 0))

    outs = [jax.ShapeDtypeStruct((members, k_size, cut, x_size), F32) for cut in cuts]
    smem = pl.BlockSpec(memory_space=pltpu.SMEM)
    return pl.pallas_call(
        body,
        grid=(k_size,),
        in_specs=[block(b.shape[2]) for b in blocks]
        + [whole(t.shape) for t in tables]
        + [whole((1, length)), whole((length, 1)), smem, smem],
        out_specs=[block(cut) for cut in cuts],
        out_shape=outs,
        compiler_params=params(),
        cost_estimate=cost(8 * triple * length * length * k_size, [*blocks, *outs]),
    )(
        *blocks,
        *tables,
        eig_x.reshape(1, length),
        eig_y.reshape(length, 1),
        eig_z,
        shift.reshape(1),
    )


def z_out(blocks, table, column, shape, earlier, first):
    members, part, y_size, x_size = blocks.shape
    triple, length = table.shape
    tiles, rows, skip = length // LANES, members * part, first // ROWS

    def body(*refs):
        flat = refs[0].reshape(rows * ROWS, x_size)
        tab, out, turned = refs[1], refs[-2], refs[-1]
        for y in range(0, ROWS, 2):
            pair = jnp.concatenate(
                [flat[pl.ds(y + d, rows, stride=ROWS), :] for d in range(2)], axis=1
            )
            done = contract(data_parts(pair.T, 1), tab[...])
            for d in range(2):
                for t in range(tiles):
                    turned[t, pl.ds(y + d, x_size, stride=ROWS), :] = done[
                        d * x_size : (d + 1) * x_size, t * LANES : (t + 1) * LANES
                    ]
        for t in range(tiles):
            out[0, :, :, t * LANES : (t + 1) * LANES] = turned[t].reshape(
                x_size, ROWS, LANES
            )

    given = [] if earlier is None else [earlier]
    return pl.pallas_call(
        body,
        grid=(y_size // ROWS,),
        in_specs=[
            pl.BlockSpec((members, part, ROWS, x_size), lambda i: (0, 0, i, 0)),
            whole(table.shape),
        ]
        + [pl.BlockSpec(memory_space=pl.ANY)] * len(given),
        out_specs=pl.BlockSpec(
            (1, x_size, ROWS, length), lambda i: (column, 0, i + skip, 0)
        ),
        out_shape=jax.ShapeDtypeStruct(shape, F32),
        scratch_shapes=[pltpu.VMEM((tiles, x_size * ROWS, LANES), F32)],
        input_output_aliases={2: 0} if given else {},
        compiler_params=params(),
        cost_estimate=cost(2 * triple * length * x_size * y_size, [blocks, blocks]),
    )(blocks, table, *given)


def z_in_plain(columns, column, table, members, first, y_size):
    exact = dict(precision=lax.Precision.HIGHEST)
    volume = columns[column, :, first : first + y_size]
    done = jnp.einsum("kz,xyz->kyx", table, volume, **exact)
    return done.reshape(members, -1, *done.shape[1:])


def planes_plain(blocks, cuts, groups, tables, eig_x, eig_y, eig_z, shift):
    exact = dict(precision=lax.Precision.HIGHEST)
    blocks = jnp.concatenate(blocks, axis=2)
    y_in, x_in, x_out, y_out = tables
    members, k_size, y_size, x_size = blocks.shape
    data = blocks.reshape(groups, members // groups, k_size, y_size, x_size)
    plane = data.transpose(2, 1, 3, 0, 4).reshape(
        k_size, members // groups * y_size, groups * x_size
    )
    spectral = jnp.einsum("jy,kyx->kjx", y_in, plane, **exact)
    spectral = jnp.einsum("kjx,xi->kji", spectral, x_in, **exact)
    denominator = eig_x[None, None] + eig_y[None, :, None] + eig_z[:, None, None] + shift
    scaled = jnp.sqrt(2.0 * shift) * spectral / denominator
    back = jnp.einsum("kji,ix->kjx", scaled, x_out, **exact)
    back = jnp.einsum("yj,kjx->kyx", y_out, back, **exact)
    back = back.reshape(k_size, members // groups, y_size, groups, x_size)
    back = back.transpose(3, 1, 0, 2, 4).reshape(blocks.shape)
    return jnp.split(back, [sum(cuts[:i]) for i in range(1, len(cuts))], axis=2)


def z_out_plain(blocks, table, column, shape, earlier, first):
    exact = dict(precision=lax.Precision.HIGHEST)
    rows = blocks.reshape(-1, *blocks.shape[2:])
    done = jnp.einsum("kyx,kz->xyz", rows, table, **exact)
    result = jnp.zeros(shape, F32) if earlier is None else earlier
    return result.at[column, :, first : first + blocks.shape[2]].set(done)


def after(value, *earlier):
    return lax.optimization_barrier((value, *earlier))[0]


def per_device(
    columns,
    basis_in_x,
    basis_in_y,
    basis_in_z,
    basis_out_x,
    basis_out_y,
    basis_out_z,
    eig_x,
    eig_y,
    eig_z,
    shift_table,
    shift_index,
):
    count, x_size, y_size, length = columns.shape
    slots, groups = lax.axis_size("pen"), lax.axis_size("grp")
    members = slots * groups
    k_size = length // members
    shift = shift_table[shift_index]
    tiled = x_size % LANES == 0 and y_size % ROWS == 0 and length % LANES == 0
    parts = table_parts if tiled else lambda table, axis: table
    to_z, across, from_z = (
        (z_in, planes, z_out) if tiled else (z_in_plain, planes_plain, z_out_plain)
    )

    in_table, out_table = parts(basis_in_z, 1), parts(basis_out_z.T, 0)
    tables = [
        parts(basis_in_y, 1),
        parts(basis_in_x.T, 0),
        parts(basis_out_x.T, 0),
        parts(basis_out_y, 1),
    ]
    levels = lax.dynamic_slice_in_dim(
        eig_z, lax.axis_index(BOTH) * k_size, k_size
    )

    def exchange(blocks):
        return lax.all_to_all(blocks, BOTH, split_axis=0, concat_axis=0, tiled=True)

    end = END if tiled and y_size > END else 0
    there = []
    for c in range(count):
        cuts = [end, y_size - end] if end and c == 0 else [y_size]
        sent, first = [], 0
        for cut in cuts:
            table = after(in_table, start) if sent else in_table
            start = to_z(columns, c, table, members, first, cut)
            sent.append(exchange(after(start, sent[-1]) if sent else start))
            first += cut
        there.append(sent)
    back = []
    for c in range(count):
        cuts = [y_size - end, end] if end and c == count - 1 else [y_size]
        outs = across(there[c], cuts, groups, tables, eig_x, eig_y, levels, shift[c])
        got = []
        for out in outs:
            got.append(exchange(after(out, got[-1]) if got else out))
        back.append(got)
    result = None
    for c in range(count):
        first = 0
        for blocks in back[c]:
            result = from_z(blocks, out_table, c, columns.shape, result, first)
            first += blocks.shape[2]
    return result


def solution(mesh):
    in_specs = (P(None, "grp", "pen", None), P(), P(), P(), P(), P(), P(), P(), P(), P(), P(), P())
    out_specs = P(None, "grp", "pen", None)
    return jax.shard_map(
        per_device, mesh=mesh, in_specs=in_specs, out_specs=out_specs, check_vma=False
    )
```

```python
import jax
import jax.numpy as jnp
from jax import lax
from jax.experimental import pallas as pl
from jax.experimental.pallas import tpu as pltpu
from jax.sharding import PartitionSpec as P

LATE = 4
LANES = 128
ROWS = 8
VMEM = 56 * 2**20
F32, BF16 = jnp.float32, jnp.bfloat16
BOTH = ("grp", "pen")


def table_parts(table, axis):
    high = lax.reduce_precision(table, exponent_bits=8, mantissa_bits=7)
    low = (table - high).astype(BF16)
    high = high.astype(BF16)
    return jnp.concatenate([high, low, high], axis=axis)


def data_parts(data, axis):
    high = data.astype(BF16)
    low = (data - high.astype(F32)).astype(BF16)
    return jnp.concatenate([high, high, low], axis=axis)


def contract(a, b, dims=((1,), (0,))):
    return lax.dot_general(a, b, (dims, ((), ())), preferred_element_type=F32)


def cost(flops, arrays):
    return pl.CostEstimate(
        flops=flops, bytes_accessed=sum(4 * a.size for a in arrays), transcendentals=0
    )


def params():
    return pltpu.CompilerParams(
        dimension_semantics=("arbitrary",), vmem_limit_bytes=VMEM
    )


def whole(shape):
    return pl.BlockSpec(shape, lambda i: (0,) * len(shape))


def z_in(columns, column, table, members, first, y_size):
    _, x_size, _, length = columns.shape
    rows, triple = table.shape
    part, tiles, skip = rows // members, length // LANES, first // ROWS
    out = jax.ShapeDtypeStruct((members, part, y_size, x_size), F32)

    def body(*refs):
        flat = [r.at[0].reshape(x_size * ROWS, LANES) for r in refs[:tiles]]
        tab, out = refs[tiles], refs[tiles + 1].reshape(rows * ROWS, x_size)
        for y in range(0, ROWS, 2):
            pair = jnp.concatenate(
                [
                    jnp.concatenate(
                        [f[pl.ds(y + d, x_size, stride=ROWS), :] for f in flat], axis=1
                    )
                    for d in range(2)
                ],
                axis=0,
            )
            done = contract(tab[...], data_parts(pair, 1), ((1,), (1,)))
            for d in range(2):
                out[pl.ds(y + d, rows, stride=ROWS), :] = done[
                    :, d * x_size : (d + 1) * x_size
                ]

    def tile(t):
        return pl.BlockSpec(
            (1, x_size, ROWS, LANES), lambda i: (column, 0, i + skip, t)
        )

    return pl.pallas_call(
        body,
        grid=(y_size // ROWS,),
        in_specs=[tile(t) for t in range(tiles)] + [whole(table.shape)],
        out_specs=pl.BlockSpec((members, part, ROWS, x_size), lambda i: (0, 0, i, 0)),
        out_shape=out,
        compiler_params=params(),
        cost_estimate=cost(2 * rows * triple * x_size * y_size, [out, out]),
    )(*[columns] * tiles, table)


def z_in_first(columns, table, me, groups, slots):
    _, x_size, _, length = columns.shape
    k_size, tiles = length // (groups * slots), length // LANES
    share = groups * k_size
    outs = [jax.ShapeDtypeStruct((groups, k_size, ROWS, x_size), F32)] * slots

    def body(*refs):
        flat = [r.at[0].reshape(x_size * ROWS, LANES) for r in refs[:tiles]]
        tab, place = refs[tiles], refs[tiles + 1]
        out = [r.reshape(share * ROWS, x_size) for r in refs[tiles + 2 :]]

        def row(s, t):
            member = (place[0] ^ t) * slots + (place[1] ^ s)
            return pl.multiple_of(member * k_size, ROWS)

        ordered = jnp.concatenate(
            [
                tab[pl.ds(row(s, t), k_size), :]
                for s in range(slots)
                for t in range(groups)
            ],
            axis=0,
        )
        high = ordered.astype(BF16)
        low = (ordered - high.astype(F32)).astype(BF16)
        ordered = jnp.concatenate([high, low, high], axis=1)
        for y in range(0, ROWS, 2):
            pair = jnp.concatenate(
                [
                    jnp.concatenate(
                        [f[pl.ds(y + d, x_size, stride=ROWS), :] for f in flat], axis=1
                    )
                    for d in range(2)
                ],
                axis=0,
            )
            done = contract(ordered, data_parts(pair, 1), ((1,), (1,)))
            for n, o in enumerate(out):
                for d in range(2):
                    o[pl.ds(y + d, share, stride=ROWS), :] = done[
                        n * share : (n + 1) * share, d * x_size : (d + 1) * x_size
                    ]

    def tile(t):
        return pl.BlockSpec((1, x_size, ROWS, LANES), lambda i: (0, 0, 0, t))

    return pl.pallas_call(
        body,
        grid=(1,),
        in_specs=[tile(t) for t in range(tiles)]
        + [whole(table.shape), pl.BlockSpec(memory_space=pltpu.SMEM)],
        out_specs=[whole(o.shape) for o in outs],
        out_shape=outs,
        compiler_params=params(),
        cost_estimate=cost(6 * length * length * x_size * ROWS, [*outs, *outs]),
    )(*[columns] * tiles, table, me)


def planes(blocks, cuts, slotted, me, groups, tables, eig_x, eig_y, eig_z, shift):
    members, k_size, _, x_size = blocks[0].shape
    slots, count = members // groups, len(blocks)
    y_size = sum(b.shape[2] for b in blocks)
    length = slots * y_size
    triple = 3 * length

    def body(*refs):
        data, out = refs[:count], refs[count + 9 :]
        y_in, x_in, x_out, y_out, ex, ey, ez, sh, place = refs[count : count + 9]

        def index(g, p, size):
            if size in slotted:
                return (place[0] ^ g) * slots + (place[1] ^ p)
            return g * slots + p

        plane = jnp.concatenate(
            [
                jnp.concatenate(
                    [
                        d[index(g, p, d.shape[2]), 0]
                        for p in range(slots)
                        for d in data
                    ],
                    axis=0,
                )
                for g in range(groups)
            ],
            axis=1,
        )
        spectral = contract(y_in[...], data_parts(plane, 0))
        spectral = contract(data_parts(spectral, 1), x_in[...])
        value = sh[0]
        root = jnp.sqrt(2.0 * jnp.full((1, length), value, F32))
        denominator = (ex[...] + ey[...]) + (ez[pl.program_id(0)] + value)
        scaled = root * spectral / denominator
        back = contract(data_parts(scaled, 1), x_out[...])
        back = contract(y_out[...], data_parts(back, 0))
        for g in range(groups):
            for p in range(slots):
                start = p * y_size
                for o, cut in zip(out, cuts):
                    o[index(g, p, cut), 0] = back[
                        start : start + cut, g * x_size : (g + 1) * x_size
                    ]
                    start += cut

    def block(cut):
        return pl.BlockSpec((members, 1, cut, x_size), lambda i: (0, i, 0, 0))

    outs = [jax.ShapeDtypeStruct((members, k_size, cut, x_size), F32) for cut in cuts]
    smem = pl.BlockSpec(memory_space=pltpu.SMEM)
    return pl.pallas_call(
        body,
        grid=(k_size,),
        in_specs=[block(b.shape[2]) for b in blocks]
        + [whole(t.shape) for t in tables]
        + [whole((1, length)), whole((length, 1)), smem, smem, smem],
        out_specs=[block(cut) for cut in cuts],
        out_shape=outs,
        compiler_params=params(),
        cost_estimate=cost(8 * triple * length * length * k_size, [*blocks, *outs]),
    )(
        *blocks,
        *tables,
        eig_x.reshape(1, length),
        eig_y.reshape(length, 1),
        eig_z,
        shift.reshape(1),
        me,
    )


def z_out(blocks, table, column, shape, earlier, first):
    count = len(blocks)
    members, part, y_size, x_size = blocks[0].shape
    triple, length = table.shape
    tiles, rows, skip = length // LANES, members * part, first // ROWS

    def body(*refs):
        flat = [r.reshape(rows * ROWS, x_size) for r in refs[:count]]
        tab, out, turned = refs[count], refs[-2], refs[-1]
        for y in range(0, ROWS, 2):
            pair = jnp.concatenate(
                [
                    jnp.concatenate(
                        [f[pl.ds(y + d, rows, stride=ROWS), :] for f in flat], axis=0
                    )
                    for d in range(2)
                ],
                axis=1,
            )
            done = contract(data_parts(pair.T, 1), tab[...])
            for d in range(2):
                for t in range(tiles):
                    turned[t, pl.ds(y + d, x_size, stride=ROWS), :] = done[
                        d * x_size : (d + 1) * x_size, t * LANES : (t + 1) * LANES
                    ]
        for t in range(tiles):
            out[0, :, :, t * LANES : (t + 1) * LANES] = turned[t].reshape(
                x_size, ROWS, LANES
            )

    given = [] if earlier is None else [earlier]
    return pl.pallas_call(
        body,
        grid=(y_size // ROWS,),
        in_specs=[pl.BlockSpec((members, part, ROWS, x_size), lambda i: (0, 0, i, 0))]
        * count
        + [whole(table.shape)]
        + [pl.BlockSpec(memory_space=pl.ANY)] * len(given),
        out_specs=pl.BlockSpec(
            (1, x_size, ROWS, length), lambda i: (column, 0, i + skip, 0)
        ),
        out_shape=jax.ShapeDtypeStruct(shape, F32),
        scratch_shapes=[pltpu.VMEM((tiles, x_size * ROWS, LANES), F32)],
        input_output_aliases={count + 1: 0} if given else {},
        compiler_params=params(),
        cost_estimate=cost(2 * triple * length * x_size * y_size, [*blocks, *blocks]),
    )(*blocks, table, *given)


def z_in_plain(columns, column, table, members, first, y_size):
    exact = dict(precision=lax.Precision.HIGHEST)
    volume = columns[column, :, first : first + y_size]
    done = jnp.einsum("kz,xyz->kyx", table, volume, **exact)
    return done.reshape(members, -1, *done.shape[1:])


def planes_plain(blocks, cuts, slotted, me, groups, tables, eig_x, eig_y, eig_z, shift):
    exact = dict(precision=lax.Precision.HIGHEST)
    blocks = jnp.concatenate(blocks, axis=2)
    y_in, x_in, x_out, y_out = tables
    members, k_size, y_size, x_size = blocks.shape
    data = blocks.reshape(groups, members // groups, k_size, y_size, x_size)
    plane = data.transpose(2, 1, 3, 0, 4).reshape(
        k_size, members // groups * y_size, groups * x_size
    )
    spectral = jnp.einsum("jy,kyx->kjx", y_in, plane, **exact)
    spectral = jnp.einsum("kjx,xi->kji", spectral, x_in, **exact)
    denominator = eig_x[None, None] + eig_y[None, :, None] + eig_z[:, None, None] + shift
    scaled = jnp.sqrt(2.0 * shift) * spectral / denominator
    back = jnp.einsum("kji,ix->kjx", scaled, x_out, **exact)
    back = jnp.einsum("yj,kjx->kyx", y_out, back, **exact)
    back = back.reshape(k_size, members // groups, y_size, groups, x_size)
    back = back.transpose(3, 1, 0, 2, 4).reshape(blocks.shape)
    return jnp.split(back, [sum(cuts[:i]) for i in range(1, len(cuts))], axis=2)


def z_out_plain(blocks, table, column, shape, earlier, first):
    exact = dict(precision=lax.Precision.HIGHEST)
    (blocks,) = blocks
    rows = blocks.reshape(-1, *blocks.shape[2:])
    done = jnp.einsum("kyx,kz->xyz", rows, table, **exact)
    result = jnp.zeros(shape, F32) if earlier is None else earlier
    return result.at[column, :, first : first + blocks.shape[2]].set(done)


def after(value, *earlier):
    return lax.optimization_barrier((value, *earlier))[0]


def slot_order(table, axis, mesh_axis):
    order = lax.axis_index(mesh_axis) ^ jnp.arange(lax.axis_size(mesh_axis))
    return jnp.take(table, order, axis=axis, mode="clip")


def swap(blocks, axis):
    size = len(blocks)
    far = sorted(range(1, size), key=lambda s: s < size // 2)
    got = {0: blocks[0]}
    for s in far:
        got[s] = lax.ppermute(blocks[s], axis, [(m, m ^ s) for m in range(size)])
    return [got[s] for s in range(size)]


def turn(blocks):
    return [jnp.stack([b[n] for b in blocks]) for n in range(blocks[0].shape[0])]


def per_device(
    columns,
    basis_in_x,
    basis_in_y,
    basis_in_z,
    basis_out_x,
    basis_out_y,
    basis_out_z,
    eig_x,
    eig_y,
    eig_z,
    shift_table,
    shift_index,
):
    count, x_size, y_size, length = columns.shape
    slots, groups = lax.axis_size("pen"), lax.axis_size("grp")
    members = slots * groups
    k_size = length // members
    shift = shift_table[shift_index]
    tiled = x_size % LANES == 0 and y_size % ROWS == 0 and length % LANES == 0
    parts = table_parts if tiled else lambda table, axis: table
    to_z, across, from_z = (
        (z_in, planes, z_out) if tiled else (z_in_plain, planes_plain, z_out_plain)
    )

    in_table, out_table = parts(basis_in_z, 1), parts(basis_out_z.T, 0)
    tables = [
        parts(basis_in_y, 1),
        parts(basis_in_x.T, 0),
        parts(basis_out_x.T, 0),
        parts(basis_out_y, 1),
    ]

    def by_member(table):
        table = table.reshape(groups, slots, k_size, length)
        table = slot_order(slot_order(table, 0, "grp"), 1, "pen")
        return table.transpose(1, 0, 2, 3).reshape(length, length)

    slot_out_table = parts(by_member(basis_out_z.T), 0)
    me = jnp.stack([lax.axis_index("grp"), lax.axis_index("pen")])
    levels = lax.dynamic_slice_in_dim(
        eig_z, lax.axis_index(BOTH) * k_size, k_size
    )

    def exchange(block):
        return lax.all_to_all(block, BOTH, split_axis=0, concat_axis=0, tiled=True)

    end = ROWS if tiled and y_size > ROWS and k_size % ROWS == 0 else 0
    there, previous = [], None
    for c in range(count):
        blocks, first = [], 0
        if end and c == 0:
            small = z_in_first(columns, basis_in_z, me, groups, slots)
            small = swap(small, "pen")
            previous = small[1:]
            small = swap(turn(small), "grp")
            blocks, first = [jnp.concatenate(small)], end
        table = after(in_table, *small[1:]) if end and c == 1 else in_table
        out = to_z(columns, c, table, members, first, y_size - first)
        out = exchange(after(out, *previous) if previous else out)
        previous = [out]
        there.append([*blocks, out])
    back, previous = [], None
    for c in range(count):
        cuts = [end, y_size - end] if end and c == count - 1 else [y_size]
        outs = across(
            there[c], cuts, [end], me, groups, tables, eig_x, eig_y, levels, shift[c]
        )
        out = exchange(after(outs[-1], *previous) if previous else outs[-1])
        previous = [out]
        back.append([(y_size - cuts[-1], [out], out_table)])
        if len(cuts) > 1:
            small = outs[0].reshape(groups, slots, *outs[0].shape[1:])
            small = turn(swap([small[t] for t in range(groups)], "grp"))
            late = slots - slots // LATE
            small = swap(
                [after(b, out) if s >= late else b for s, b in enumerate(small)], "pen"
            )
            back[c].append((0, small, slot_out_table))
    result = None
    for c in range(count):
        for first, blocks, table in back[c]:
            result = from_z(blocks, table, c, columns.shape, result, first)
    return result


def solution(mesh):
    in_specs = (P(None, "grp", "pen", None), P(), P(), P(), P(), P(), P(), P(), P(), P(), P(), P())
    out_specs = P(None, "grp", "pen", None)
    return jax.shard_map(
        per_device, mesh=mesh, in_specs=in_specs, out_specs=out_specs, check_vma=False
    )
```

```python
import jax
import jax.numpy as jnp
from jax import lax
from jax.experimental import pallas as pl
from jax.experimental.pallas import tpu as pltpu
from jax.sharding import PartitionSpec as P

LATE = 4
LANES = 128
ROWS = 8
VMEM = 56 * 2**20
F32, BF16 = jnp.float32, jnp.bfloat16
BOTH = ("grp", "pen")


def table_parts(table, axis):
    high = lax.reduce_precision(table, exponent_bits=8, mantissa_bits=7)
    low = (table - high).astype(BF16)
    high = high.astype(BF16)
    return jnp.concatenate([high, low, high], axis=axis)


def data_parts(data, axis):
    high = data.astype(BF16)
    low = (data - high.astype(F32)).astype(BF16)
    return jnp.concatenate([high, high, low], axis=axis)


def contract(a, b, dims=((1,), (0,))):
    return lax.dot_general(a, b, (dims, ((), ())), preferred_element_type=F32)


def cost(flops, arrays):
    return pl.CostEstimate(
        flops=flops, bytes_accessed=sum(4 * a.size for a in arrays), transcendentals=0
    )


def params():
    return pltpu.CompilerParams(
        dimension_semantics=("arbitrary",), vmem_limit_bytes=VMEM
    )


def whole(shape):
    return pl.BlockSpec(shape, lambda i: (0,) * len(shape))


def z_in(columns, column, table, members, first, y_size):
    _, x_size, _, length = columns.shape
    rows, triple = table.shape
    part, tiles, skip = rows // members, length // LANES, first // ROWS
    out = jax.ShapeDtypeStruct((members, part, y_size, x_size), F32)

    def body(*refs):
        flat = [r.at[0].reshape(x_size * ROWS, LANES) for r in refs[:tiles]]
        tab, out = refs[tiles], refs[tiles + 1].reshape(rows * ROWS, x_size)
        for y in range(0, ROWS, 2):
            pair = jnp.concatenate(
                [
                    jnp.concatenate(
                        [f[pl.ds(y + d, x_size, stride=ROWS), :] for f in flat], axis=1
                    )
                    for d in range(2)
                ],
                axis=0,
            )
            done = contract(tab[...], data_parts(pair, 1), ((1,), (1,)))
            for d in range(2):
                out[pl.ds(y + d, rows, stride=ROWS), :] = done[
                    :, d * x_size : (d + 1) * x_size
                ]

    def tile(t):
        return pl.BlockSpec(
            (1, x_size, ROWS, LANES), lambda i: (column, 0, i + skip, t)
        )

    return pl.pallas_call(
        body,
        grid=(y_size // ROWS,),
        in_specs=[tile(t) for t in range(tiles)] + [whole(table.shape)],
        out_specs=pl.BlockSpec((members, part, ROWS, x_size), lambda i: (0, 0, i, 0)),
        out_shape=out,
        compiler_params=params(),
        cost_estimate=cost(2 * rows * triple * x_size * y_size, [out, out]),
    )(*[columns] * tiles, table)


def z_in_first(columns, table, me, groups, slots):
    _, x_size, _, length = columns.shape
    k_size, tiles = length // (groups * slots), length // LANES
    share = groups * k_size
    outs = [jax.ShapeDtypeStruct((groups, k_size, ROWS, x_size), F32)] * slots

    def body(*refs):
        flat = [r.at[0].reshape(x_size * ROWS, LANES) for r in refs[:tiles]]
        tab, place = refs[tiles], refs[tiles + 1]
        out = [r.reshape(share * ROWS, x_size) for r in refs[tiles + 2 :]]

        def row(s, t):
            member = (place[0] ^ t) * slots + (place[1] ^ s)
            return pl.multiple_of(member * k_size, ROWS)

        ordered = jnp.concatenate(
            [
                tab[pl.ds(row(s, t), k_size), :]
                for s in range(slots)
                for t in range(groups)
            ],
            axis=0,
        )
        high = ordered.astype(BF16)
        low = (ordered - high.astype(F32)).astype(BF16)
        ordered = jnp.concatenate([high, low, high], axis=1)
        for y in range(0, ROWS, 2):
            pair = jnp.concatenate(
                [
                    jnp.concatenate(
                        [f[pl.ds(y + d, x_size, stride=ROWS), :] for f in flat], axis=1
                    )
                    for d in range(2)
                ],
                axis=0,
            )
            done = contract(ordered, data_parts(pair, 1), ((1,), (1,)))
            for n, o in enumerate(out):
                for d in range(2):
                    o[pl.ds(y + d, share, stride=ROWS), :] = done[
                        n * share : (n + 1) * share, d * x_size : (d + 1) * x_size
                    ]

    def tile(t):
        return pl.BlockSpec((1, x_size, ROWS, LANES), lambda i: (0, 0, 0, t))

    return pl.pallas_call(
        body,
        grid=(1,),
        in_specs=[tile(t) for t in range(tiles)]
        + [whole(table.shape), pl.BlockSpec(memory_space=pltpu.SMEM)],
        out_specs=[whole(o.shape) for o in outs],
        out_shape=outs,
        compiler_params=params(),
        cost_estimate=cost(6 * length * length * x_size * ROWS, [*outs, *outs]),
    )(*[columns] * tiles, table, me)


def planes(blocks, cuts, slotted, me, groups, tables, eig_x, eig_y, eig_z, shift):
    members, k_size, _, x_size = blocks[0].shape
    slots, count = members // groups, len(blocks)
    y_size = sum(b.shape[2] for b in blocks)
    length = slots * y_size
    triple = 3 * length

    def body(*refs):
        data, out = refs[:count], refs[count + 9 :]
        y_in, x_in, x_out, y_out, ex, ey, ez, sh, place = refs[count : count + 9]

        def index(g, p, size):
            if size in slotted:
                return (place[0] ^ g) * slots + (place[1] ^ p)
            return g * slots + p

        plane = jnp.concatenate(
            [
                jnp.concatenate(
                    [
                        d[index(g, p, d.shape[2]), 0]
                        for p in range(slots)
                        for d in data
                    ],
                    axis=0,
                )
                for g in range(groups)
            ],
            axis=1,
        )
        spectral = contract(y_in[...], data_parts(plane, 0))
        spectral = contract(data_parts(spectral, 1), x_in[...])
        value = sh[0]
        root = jnp.sqrt(2.0 * jnp.full((1, length), value, F32))
        denominator = (ex[...] + ey[...]) + (ez[pl.program_id(0)] + value)
        scaled = root * spectral / denominator
        back = contract(data_parts(scaled, 1), x_out[...])
        back = contract(y_out[...], data_parts(back, 0))
        for g in range(groups):
            for p in range(slots):
                start = p * y_size
                for o, cut in zip(out, cuts):
                    o[index(g, p, cut), 0] = back[
                        start : start + cut, g * x_size : (g + 1) * x_size
                    ]
                    start += cut

    def block(cut):
        return pl.BlockSpec((members, 1, cut, x_size), lambda i: (0, i, 0, 0))

    outs = [jax.ShapeDtypeStruct((members, k_size, cut, x_size), F32) for cut in cuts]
    smem = pl.BlockSpec(memory_space=pltpu.SMEM)
    return pl.pallas_call(
        body,
        grid=(k_size,),
        in_specs=[block(b.shape[2]) for b in blocks]
        + [whole(t.shape) for t in tables]
        + [whole((1, length)), whole((length, 1)), smem, smem, smem],
        out_specs=[block(cut) for cut in cuts],
        out_shape=outs,
        compiler_params=params(),
        cost_estimate=cost(8 * triple * length * length * k_size, [*blocks, *outs]),
    )(
        *blocks,
        *tables,
        eig_x.reshape(1, length),
        eig_y.reshape(length, 1),
        eig_z,
        shift.reshape(1),
        me,
    )


def z_out(blocks, table, column, shape, earlier, first):
    count = len(blocks)
    members, part, y_size, x_size = blocks[0].shape
    triple, length = table.shape
    tiles, rows, skip = length // LANES, members * part, first // ROWS

    def body(*refs):
        flat = [r.reshape(rows * ROWS, x_size) for r in refs[:count]]
        tab, out, turned = refs[count], refs[-2], refs[-1]
        for y in range(0, ROWS, 2):
            pair = jnp.concatenate(
                [
                    jnp.concatenate(
                        [f[pl.ds(y + d, rows, stride=ROWS), :] for f in flat], axis=0
                    )
                    for d in range(2)
                ],
                axis=1,
            )
            done = contract(data_parts(pair.T, 1), tab[...])
            for d in range(2):
                for t in range(tiles):
                    turned[t, pl.ds(y + d, x_size, stride=ROWS), :] = done[
                        d * x_size : (d + 1) * x_size, t * LANES : (t + 1) * LANES
                    ]
        for t in range(tiles):
            out[0, :, :, t * LANES : (t + 1) * LANES] = turned[t].reshape(
                x_size, ROWS, LANES
            )

    given = [] if earlier is None else [earlier]
    return pl.pallas_call(
        body,
        grid=(y_size // ROWS,),
        in_specs=[pl.BlockSpec((members, part, ROWS, x_size), lambda i: (0, 0, i, 0))]
        * count
        + [whole(table.shape)]
        + [pl.BlockSpec(memory_space=pl.ANY)] * len(given),
        out_specs=pl.BlockSpec(
            (1, x_size, ROWS, length), lambda i: (column, 0, i + skip, 0)
        ),
        out_shape=jax.ShapeDtypeStruct(shape, F32),
        scratch_shapes=[pltpu.VMEM((tiles, x_size * ROWS, LANES), F32)],
        input_output_aliases={count + 1: 0} if given else {},
        compiler_params=params(),
        cost_estimate=cost(2 * triple * length * x_size * y_size, [*blocks, *blocks]),
    )(*blocks, table, *given)


def z_in_plain(columns, column, table, members, first, y_size):
    exact = dict(precision=lax.Precision.HIGHEST)
    volume = columns[column, :, first : first + y_size]
    done = jnp.einsum("kz,xyz->kyx", table, volume, **exact)
    return done.reshape(members, -1, *done.shape[1:])


def planes_plain(blocks, cuts, slotted, me, groups, tables, eig_x, eig_y, eig_z, shift):
    exact = dict(precision=lax.Precision.HIGHEST)
    blocks = jnp.concatenate(blocks, axis=2)
    y_in, x_in, x_out, y_out = tables
    members, k_size, y_size, x_size = blocks.shape
    data = blocks.reshape(groups, members // groups, k_size, y_size, x_size)
    plane = data.transpose(2, 1, 3, 0, 4).reshape(
        k_size, members // groups * y_size, groups * x_size
    )
    spectral = jnp.einsum("jy,kyx->kjx", y_in, plane, **exact)
    spectral = jnp.einsum("kjx,xi->kji", spectral, x_in, **exact)
    denominator = eig_x[None, None] + eig_y[None, :, None] + eig_z[:, None, None] + shift
    scaled = jnp.sqrt(2.0 * shift) * spectral / denominator
    back = jnp.einsum("kji,ix->kjx", scaled, x_out, **exact)
    back = jnp.einsum("yj,kjx->kyx", y_out, back, **exact)
    back = back.reshape(k_size, members // groups, y_size, groups, x_size)
    back = back.transpose(3, 1, 0, 2, 4).reshape(blocks.shape)
    return jnp.split(back, [sum(cuts[:i]) for i in range(1, len(cuts))], axis=2)


def z_out_plain(blocks, table, column, shape, earlier, first):
    exact = dict(precision=lax.Precision.HIGHEST)
    (blocks,) = blocks
    rows = blocks.reshape(-1, *blocks.shape[2:])
    done = jnp.einsum("kyx,kz->xyz", rows, table, **exact)
    result = jnp.zeros(shape, F32) if earlier is None else earlier
    return result.at[column, :, first : first + blocks.shape[2]].set(done)


def after(value, *earlier):
    return lax.optimization_barrier((value, *earlier))[0]


def slot_order(table, axis, mesh_axis):
    order = lax.axis_index(mesh_axis) ^ jnp.arange(lax.axis_size(mesh_axis))
    return jnp.take(table, order, axis=axis, mode="clip")


def swap(blocks, axis):
    size = len(blocks)
    far = sorted(range(1, size), key=lambda s: s < size // 2)
    got = {0: blocks[0]}
    for s in far:
        got[s] = lax.ppermute(blocks[s], axis, [(m, m ^ s) for m in range(size)])
    return [got[s] for s in range(size)]


def turn(blocks):
    return [jnp.stack([b[n] for b in blocks]) for n in range(blocks[0].shape[0])]


def per_device(
    columns,
    basis_in_x,
    basis_in_y,
    basis_in_z,
    basis_out_x,
    basis_out_y,
    basis_out_z,
    eig_x,
    eig_y,
    eig_z,
    shift_table,
    shift_index,
):
    count, x_size, y_size, length = columns.shape
    slots, groups = lax.axis_size("pen"), lax.axis_size("grp")
    members = slots * groups
    k_size = length // members
    shift = shift_table[shift_index]
    tiled = x_size % LANES == 0 and y_size % ROWS == 0 and length % LANES == 0
    parts = table_parts if tiled else lambda table, axis: table
    to_z, across, from_z = (
        (z_in, planes, z_out) if tiled else (z_in_plain, planes_plain, z_out_plain)
    )

    in_table, out_table = parts(basis_in_z, 1), parts(basis_out_z.T, 0)
    tables = [
        parts(basis_in_y, 1),
        parts(basis_in_x.T, 0),
        parts(basis_out_x.T, 0),
        parts(basis_out_y, 1),
    ]

    def by_member(table):
        table = table.reshape(groups, slots, k_size, length)
        table = slot_order(slot_order(table, 0, "grp"), 1, "pen")
        return table.transpose(1, 0, 2, 3).reshape(length, length)

    slot_out_table = parts(by_member(basis_out_z.T), 0)
    me = jnp.stack([lax.axis_index("grp"), lax.axis_index("pen")])
    levels = lax.dynamic_slice_in_dim(
        eig_z, lax.axis_index(BOTH) * k_size, k_size
    )

    def exchange(block):
        return lax.all_to_all(block, BOTH, split_axis=0, concat_axis=0, tiled=True)

    end = ROWS if tiled and y_size > ROWS and k_size % ROWS == 0 else 0
    order = [*range(1, count), 0]
    there, previous, small = {}, None, None
    if end:
        small = swap(z_in_first(columns, basis_in_z, me, groups, slots), "pen")
        previous = small[1 : slots - slots // LATE]
    for c in order:
        first = end if c == 0 else 0
        out = to_z(columns, c, in_table, members, first, y_size - first)
        out = exchange(after(out, *previous) if previous else out)
        previous = [out]
        there[c] = [out]
    if end:
        there[0].insert(0, jnp.concatenate(swap(turn(small), "grp")))
    back, previous = {}, None
    for c in order:
        cuts = [end, y_size - end] if end and c == 0 else [y_size]
        outs = across(
            there[c], cuts, [end], me, groups, tables, eig_x, eig_y, levels, shift[c]
        )
        out = exchange(after(outs[-1], *previous) if previous else outs[-1])
        previous = [out]
        back[c] = [(y_size - cuts[-1], [out], out_table)]
        if len(cuts) > 1:
            small = outs[0].reshape(groups, slots, *outs[0].shape[1:])
            small = turn(swap([small[t] for t in range(groups)], "grp"))
            late = slots - slots // LATE
            small = swap(
                [after(b, out) if s >= late else b for s, b in enumerate(small)], "pen"
            )
            back[c].append((0, small, slot_out_table))
    result = None
    for c in order:
        for first, blocks, table in back[c]:
            result = from_z(blocks, table, c, columns.shape, result, first)
    return result


def solution(mesh):
    in_specs = (P(None, "grp", "pen", None), P(), P(), P(), P(), P(), P(), P(), P(), P(), P(), P())
    out_specs = P(None, "grp", "pen", None)
    return jax.shard_map(
        per_device, mesh=mesh, in_specs=in_specs, out_specs=out_specs, check_vma=False
    )
```
